32 devices in a mesh: node: 4 (over y, x), local: 8 (over z, core).
Axes of the slice: x: 2, y: 2, z: 4, core: 2. Of those that a mesh axis runs over, the one named last changes fastest.
Arguments:
- grads: bfloat16 [4, 8, 2, 64, 14848], P('node', 'local'), may hold values from -0.29882812 to 0.29882812
- first_scales: bfloat16 [4, 8, 14848], P('node', 'local'), may hold values from 0.00390625 to 0.03125, as said below
- second_scales: bfloat16 [4, 14848], P('node', 'local'), may hold values from 0.00390625 to 0.015625, as said below
- param: float32 [8, 4, 464, 128], P('local', 'node'), may hold values from -6 to 6
- first_moment: float32 [8, 4, 464, 128], P('local', 'node'), may hold values from -3 to 3
- second_moment: float32 [8, 4, 464, 128], P('local', 'node'), may hold values from 0.01 to 1
Outputs:
- grad_sum: float32 [8, 4, 464, 128], P('local', 'node')
- new_param: float32 [8, 4, 464, 128], P('local', 'node')
- new_first: float32 [8, 4, 464, 128], P('local', 'node')
- new_second: float32 [8, 4, 464, 128], P('local', 'node')
The draws below stay inside these ranges and needn't reach their ends.
Inputs may be any that keep to these rules, and one draw needn't show every extreme that they name: `first_scales`: every entry is a power of two. `second_scales`: every entry is a power of two.
All inputs are finite; a program needn't handle non-finite values.
Results may differ from the reference program's by a relative error of at most 0.0014.
Values may be sent and summed in bfloat16 or wider, within the bound.
A program may use at most 64 MiB of HBM per device.

```python
import math
import jax
import jax.numpy as jnp
from jax import lax

D = 14848
BS = 128
LAYERS = 2
ROWS = 64
NB = 14848
OWN = 464
N_NODE = 4
N_LOCAL = 8


def draw_first_scales(key, part):
    key = jax.random.fold_in(key, 11)
    picks = jax.random.randint(key, (N_NODE, N_LOCAL, NB), 0, 4)
    table = jnp.array([2.0 ** (-8), 2.0 ** (-7), 2.0 ** (-6), 2.0 ** (-5)], jnp.float32)
    return table[picks].astype(jnp.bfloat16)


def draw_second_scales(key, part):
    key = jax.random.fold_in(key, 23)
    picks = jax.random.randint(key, (N_NODE, NB), 0, 3)
    table = jnp.array([2.0 ** (-8), 2.0 ** (-7), 2.0 ** (-6)], jnp.float32)
    return table[picks].astype(jnp.bfloat16)


def block_levels(stream_key, dims, pieces, least, high):
    def one(axis_at, shards_of):
        steps = jax.random.uniform(jax.random.fold_in(jax.random.fold_in(stream_key, 6), axis_at), (shards_of,), jnp.float32, least / len(pieces), high / len(pieces))
        return jnp.repeat(jnp.exp(steps), dims[axis_at] // shards_of).reshape((-1,) + (1,) * (len(dims) - axis_at - 1))

    factor_of = one(*pieces[0])
    for cut in pieces[1:]:
        factor_of = factor_of * one(*cut)
    return factor_of


def noise(rng, extent, spread, reach, shards=(), held_as=jnp.bfloat16):
    loudness = block_levels(rng, extent, shards, -0.22, 0.18) if shards else 1.0
    result = jax.random.normal(rng, extent, jnp.float32) * spread * loudness
    return jnp.minimum(jnp.maximum(result, -reach), reach).astype(held_as)


def setup_inputs(seed: int = 0) -> dict:
    streams_of = jax.random.split(jax.random.key(seed), 7)
    return {
        "grads": noise(streams_of[0], (N_NODE, N_LOCAL, LAYERS, ROWS, D), 0.05, 0.29882812, ((0, 4), (1, 8))),
        "first_scales": draw_first_scales(jax.random.fold_in(streams_of[6], 71), 0),
        "second_scales": draw_second_scales(jax.random.fold_in(streams_of[6], 71), 0),
        "param": noise(streams_of[3], (N_LOCAL, N_NODE, OWN, BS), 1.0, 6.0, ((0, 8), (1, 4)), jnp.float32),
        "first_moment": noise(streams_of[4], (N_LOCAL, N_NODE, OWN, BS), 0.5, 3.0, ((0, 8), (1, 4)), jnp.float32),
        "second_moment": jnp.clip(jnp.exp(math.log(1.0) - 4.6051702 * jax.random.uniform(streams_of[5], (N_LOCAL, N_NODE, OWN, BS), jnp.float32) ** block_levels(streams_of[5], (N_LOCAL, N_NODE, OWN, BS), ((0, 8), (1, 4)), -0.2, 0.2)), 0.01, 1.0),
    }


beta_one = 0.9
beta_two = 0.999
learning_rate = 0.01
correction_one = 1.0 - 0.9 ** 20
correction_two = 1.0 - 0.999 ** 20

def nearest_even(scaled):
    lifted = jnp.floor(scaled + 0.5)
    halfway = lifted - scaled == 0.5
    parity = lifted - 2.0 * jnp.floor(lifted * 0.5)
    return jnp.where(halfway & (parity == 1.0), lifted - 1.0, lifted)

def encode(values, scales, lowest, highest):
    return jnp.clip(nearest_even(values / scales), lowest, highest)

def reference(grads, first_scales, second_scales, param, first_moment, second_moment):

    def per_node(running, items):
        grad_node, scale_node, second_node = items
        values = grad_node.astype(jnp.float32).reshape(N_LOCAL, NB, BS)
        scale_one = scale_node.astype(jnp.float32)[..., None]
        sent_terms = (encode(values, scale_one, -8.0, 7.0) * scale_one).astype(jnp.bfloat16)
        sent_terms = lax.optimization_barrier(sent_terms)
        partial_value = lax.optimization_barrier(jnp.sum(sent_terms.astype(jnp.float32), axis=0))
        scale_two = second_node.astype(jnp.float32)[:, None]
        second_terms = (encode(partial_value, scale_two, -127.0, 127.0) * scale_two).astype(jnp.bfloat16)
        second_terms = lax.optimization_barrier(second_terms)
        return (running + second_terms.astype(jnp.float32), None)
    total, _ = lax.scan(per_node, jnp.zeros((NB, BS), jnp.float32), (grads, first_scales, second_scales))
    grad_sum = total.reshape(N_LOCAL, N_NODE, NB // (N_LOCAL * N_NODE), BS)
    new_first = beta_one * first_moment + (1.0 - beta_one) * grad_sum
    new_second = beta_two * second_moment + (1.0 - beta_two) * grad_sum * grad_sum
    new_param = param - learning_rate * (new_first / correction_one) / (jnp.sqrt(new_second / correction_two) + 1e-08)
    return (grad_sum, new_param, new_first, new_second)
```

```python
import functools

import jax
import jax.numpy as jnp
from jax import lax
from jax.experimental import pallas as pl
from jax.experimental.pallas import tpu as pltpu
from jax.sharding import PartitionSpec as P

beta_one = 0.9
beta_two = 0.999
learning_rate = 0.01
correction_one = 1.0 - 0.9**20
correction_two = 1.0 - 0.999**20

LANES = 128
TILE_ROWS = 16
ROUNDER = 1.5 * 2.0**23


def nearest_even(scaled):
    lifted = jnp.floor(scaled + 0.5)
    halfway = lifted - scaled == 0.5
    parity = lifted - 2.0 * jnp.floor(lifted * 0.5)
    return jnp.where(halfway & (parity == 1.0), lifted - 1.0, lifted)


def encode(values, scales, lowest, highest):
    return jnp.clip(nearest_even(values / scales), lowest, highest)


def adam(grad_sum, param, first_moment, second_moment):
    new_first = beta_one * first_moment + (1.0 - beta_one) * grad_sum
    new_second = beta_two * second_moment + (1.0 - beta_two) * grad_sum * grad_sum
    new_param = param - learning_rate * (new_first / correction_one) / (
        jnp.sqrt(new_second / correction_two) + 1e-08
    )
    return new_param, new_first, new_second


def plain_sum(grads, first_scales, second_scales, owned_blocks, block_size):
    locals_count = lax.axis_size("local")
    nodes_count = lax.axis_size("node")
    values = grads.astype(jnp.float32).reshape(locals_count, nodes_count, owned_blocks, block_size)
    scale_one = first_scales.astype(jnp.float32).reshape(locals_count, nodes_count, owned_blocks, 1)
    sent_terms = (encode(values, scale_one, -8.0, 7.0) * scale_one).astype(jnp.bfloat16)
    scale_two = second_scales.astype(jnp.float32).reshape(nodes_count, owned_blocks, 1)
    partial_value = jnp.sum(
        lax.all_to_all(sent_terms, "local", split_axis=0, concat_axis=0, tiled=True).astype(
            jnp.float32
        ),
        axis=0,
    )
    second_terms = (encode(partial_value, scale_two, -127.0, 127.0) * scale_two).astype(
        jnp.bfloat16
    )
    summed = lax.psum_scatter(second_terms, "node", scatter_dimension=0, tiled=True)
    return summed[0].astype(jnp.float32)


def round_to(values, scale, lowest, highest):
    big = scale * ROUNDER
    return jnp.clip((values + big) - big, scale * lowest, scale * highest)


def pieces_of(columns):
    fours = columns // 4
    count = min(PIECES, fours)
    sizes = [4 * (fours // count + (1 if i < fours % count else 0)) for i in range(count)]
    starts = [sum(sizes[:i]) for i in range(count)]
    return list(zip(starts, sizes))


PIECES = 4


def reduce_kernel(
    pieces,
    grads_ref,
    scale_one_ref,
    scale_two_ref,
    out_ref,
    loaded,
    cross_out,
    cross_in,
    sums,
    joined_in,
    near_in,
    far_in,
    node_out,
    node_in,
    load_sem,
    cross_send,
    cross_recv,
    half_send,
    joined_recv,
    near_recv,
    far_send,
    far_recv,
    node_send,
    node_recv,
):
    node = lax.axis_index("node")
    local = lax.axis_index("local")
    z, core = local // 2, local % 2
    half = z // 2
    inner = (z + half) % 2 == 1
    partner = z + 1 - 2 * (z % 2)
    other_inner, other_outer = 2 - half, 3 - 3 * half
    nodes = lax.axis_size("node")
    columns_of = scale_two_ref.shape[-1]
    count = len(pieces)

    def at(z_to, core_to, node_to=None):
        return (node if node_to is None else node_to, 2 * z_to + core_to)

    def destination(order):
        return jnp.where(
            order == 0,
            other_outer,
            jnp.where(order == 1, other_inner, jnp.where(order == 2, partner, z)),
        )

    def lanes(p):
        start, size = pieces[p]
        return pl.ds(start * LANES, size * LANES)

    def quarter(p):
        start, size = pieces[p]
        return pl.ds(start // 4 * LANES, size // 4 * LANES)

    barrier = pltpu.get_barrier_semaphore()
    peers = [at(z, 1 - core)]
    peers += [at((z + k) % 4, core) for k in range(1, 4)]
    peers += [(lax.rem(node + k, nodes), local) for k in range(1, 4)]
    for peer in peers:
        pl.semaphore_signal(barrier, inc=1, device_id=peer, device_id_type=pl.DeviceIdType.MESH)

    def load(order, p):
        z_to = destination(order)
        return pltpu.make_async_copy(
            grads_ref.at[pl.ds(2 * z_to, 2), :, lanes(p)],
            loaded.at[order, :, :, lanes(p)],
            load_sem.at[order, p],
        )

    for order in range(4):
        for p in range(count):
            load(order, p).start()

    def cross(order, p):
        return pltpu.make_async_remote_copy(
            src_ref=cross_out.at[order, :, lanes(p)],
            dst_ref=cross_in.at[order, :, lanes(p)],
            send_sem=cross_send.at[order, p],
            recv_sem=cross_recv.at[order, p],
            device_id=at(z, 1 - core),
            device_id_type=pl.DeviceIdType.MESH,
        )

    def to_join(order, p):
        return pltpu.make_async_remote_copy(
            src_ref=sums.at[order, :, lanes(p)],
            dst_ref=joined_in.at[order, :, lanes(p)],
            send_sem=half_send.at[order, p],
            recv_sem=joined_recv.at[order, p],
            device_id=at(partner, core),
            device_id_type=pl.DeviceIdType.MESH,
        )

    def to_near(p):
        return pltpu.make_async_remote_copy(
            src_ref=sums.at[2, :, lanes(p)],
            dst_ref=near_in.at[:, lanes(p)],
            send_sem=half_send.at[2, p],
            recv_sem=near_recv.at[p],
            device_id=at(partner, core),
            device_id_type=pl.DeviceIdType.MESH,
        )

    def to_far(order, p):
        return pltpu.make_async_remote_copy(
            src_ref=sums.at[order, :, lanes(p)],
            dst_ref=far_in.at[:, lanes(p)],
            send_sem=far_send.at[order, p],
            recv_sem=far_recv.at[p],
            device_id=at(destination(order), core),
            device_id_type=pl.DeviceIdType.MESH,
        )

    def to_node(k, p):
        other = lax.rem(node + k, nodes)
        return pltpu.make_async_remote_copy(
            src_ref=node_out.at[other, :, quarter(p)],
            dst_ref=node_in.at[k - 1, :, quarter(p)],
            send_sem=node_send.at[k - 1, p],
            recv_sem=node_recv.at[k - 1, p],
            device_id=(other, local),
            device_id_type=pl.DeviceIdType.MESH,
        )

    def code(order, p, core_to, target):
        chunk = 2 * destination(order) + core_to
        start, size = pieces[p]
        scales = scale_one_ref[chunk]
        for j in range(start, start + size):
            cols = slice(j * LANES, (j + 1) * LANES)
            scale = jnp.broadcast_to(scales[:, j : j + 1], (TILE_ROWS, LANES))
            values = loaded[order, core_to, :, cols].astype(jnp.float32)
            target[order, :, cols] = round_to(values, scale, -8.0, 7.0).astype(jnp.bfloat16)

    def pair_sum(order, p):
        cross(order, p).wait_recv()
        start, size = pieces[p]
        sums[order, :, lanes(p)] = (
            sums[order, :, lanes(p)].astype(jnp.float32)
            + cross_in[order, :, lanes(p)].astype(jnp.float32)
        ).astype(jnp.bfloat16)

        @pl.when(jnp.logical_and(order < 2, jnp.logical_not(inner)))
        def _():
            to_join(order, p).start()

        @pl.when(order == 2)
        def _():
            to_near(p).start()

    def first_phase(order, carry):
        for p in range(count):
            load(order, p).wait()
            code(order, p, 1 - core, cross_out)
            if p == 0:

                @pl.when(order == 0)
                def _():
                    pl.semaphore_wait(barrier, len(peers))

            cross(order, p).start()
            code(order, p, core, sums)
            if p > 0:
                pair_sum(order, p - 1)
            else:

                @pl.when(order > 0)
                def _():
                    pair_sum(order - 1, count - 1)

        return carry

    lax.fori_loop(0, 4, first_phase, 0)
    pair_sum(3, count - 1)

    @pl.when(inner)
    def _():
        for order in range(2):
            for p in range(count):
                to_join(order, p).wait_recv()
                sums[order, :, lanes(p)] = (
                    sums[order, :, lanes(p)].astype(jnp.float32)
                    + joined_in[order, :, lanes(p)].astype(jnp.float32)
                ).astype(jnp.bfloat16)
                to_far(order, p).start()

    scales_two = scale_two_ref[...]

    def recode(p):
        to_far(0, p).wait_recv()
        to_near(p).wait_recv()
        start, size = pieces[p]
        step = size // 4
        for k in range(step):
            terms = []
            for q in range(4):
                j = start + q * step + k
                cols = slice(j * LANES, (j + 1) * LANES)
                scale = jnp.broadcast_to(scales_two[:, j : j + 1], (TILE_ROWS, LANES))
                total = (
                    sums[3, :, cols].astype(jnp.float32)
                    + near_in[:, cols].astype(jnp.float32)
                    + far_in[:, cols].astype(jnp.float32)
                )
                terms.append(round_to(total, scale, -127.0, 127.0))
            where = slice((start // 4 + k) * LANES, (start // 4 + k + 1) * LANES)
            for n in range(4):
                node_out[n, :, where] = jnp.concatenate(
                    [term[4 * n : 4 * n + 4] for term in terms], axis=0
                ).astype(jnp.bfloat16)
        for k in range(1, 4):
            to_node(k, p).start()

    def collect(p):
        for k in range(1, 4):
            to_node(k, p).wait_recv()
        start, size = pieces[p]
        step = size // 4
        for k in range(step):
            where = slice((start // 4 + k) * LANES, (start // 4 + k + 1) * LANES)
            total = node_out[node, :, where].astype(jnp.float32)
            for i in range(3):
                total = total + node_in[i, :, where].astype(jnp.float32)
            for q in range(4):
                j = start + q * step + k
                out_ref[pl.ds(j, 4, stride=columns_of), :] = total[4 * q : 4 * q + 4]

    for p in range(count):
        recode(p)
        if p > 0:
            collect(p - 1)
    collect(count - 1)

    for p in range(count):
        for order in range(4):
            cross(order, p).wait_send()
        to_near(p).wait_send()
        for k in range(1, 4):
            to_node(k, p).wait_send()

    @pl.when(inner)
    def _():
        for p in range(count):
            for order in range(2):
                to_far(order, p).wait_send()

    @pl.when(jnp.logical_not(inner))
    def _():
        for p in range(count):
            for order in range(2):
                to_join(order, p).wait_send()


def line_sum(grads, first_scales, second_scales, owned_blocks, block_size):
    locals_count = lax.axis_size("local")
    depth = grads.shape[-1]
    columns = depth // block_size
    pieces = pieces_of(columns)
    count = len(pieces)
    rows = TILE_ROWS
    scratch = [
        pltpu.VMEM((4, 2, rows, depth), jnp.bfloat16),
        pltpu.VMEM((4, rows, depth), jnp.bfloat16),
        pltpu.VMEM((4, rows, depth), jnp.bfloat16),
        pltpu.VMEM((4, rows, depth), jnp.bfloat16),
        pltpu.VMEM((2, rows, depth), jnp.bfloat16),
        pltpu.VMEM((rows, depth), jnp.bfloat16),
        pltpu.VMEM((rows, depth), jnp.bfloat16),
        pltpu.VMEM((4, rows, depth // 4), jnp.bfloat16),
        pltpu.VMEM((3, rows, depth // 4), jnp.bfloat16),
    ]
    sems = [(4, count)] * 3
    sems += [(3, count), (2, count), (count,), (2, count), (count,), (3, count), (3, count)]
    return pl.pallas_call(
        functools.partial(reduce_kernel, pieces),
        out_shape=jax.ShapeDtypeStruct((owned_blocks, block_size), jnp.float32),
        in_specs=[
            pl.BlockSpec(memory_space=pl.ANY),
            pl.BlockSpec(memory_space=pltpu.VMEM),
            pl.BlockSpec(memory_space=pltpu.VMEM),
        ],
        out_specs=pl.BlockSpec(memory_space=pltpu.VMEM),
        scratch_shapes=scratch + [pltpu.SemaphoreType.DMA(shape) for shape in sems],
        compiler_params=pltpu.CompilerParams(
            collective_id=0, has_side_effects=True, vmem_limit_bytes=40 * 2**20
        ),
    )(
        grads.reshape(locals_count, rows, depth),
        first_scales.astype(jnp.float32).reshape(locals_count, rows, columns),
        second_scales.astype(jnp.float32).reshape(rows, columns),
    )


def shards(grads, first_scales, second_scales, param, first_moment, second_moment):
    owned_blocks, block_size = param.shape[2:]
    nodes_count, locals_count = lax.axis_size("node"), lax.axis_size("local")
    depth = grads.shape[-1]
    columns = depth // block_size
    fits = (
        nodes_count == 4
        and locals_count == 8
        and block_size == LANES
        and depth % block_size == 0
        and columns % 4 == 0
        and owned_blocks == 4 * columns
        and grads.shape[-2] % TILE_ROWS == 0
    )
    reduced = line_sum if fits else plain_sum
    grad_sum = reduced(grads, first_scales, second_scales, owned_blocks, block_size)
    grad_sum = grad_sum.reshape(1, 1, owned_blocks, block_size)
    return (grad_sum, *adam(grad_sum, param, first_moment, second_moment))


def solution(mesh):
    owned = P("local", "node", None, None)
    return jax.shard_map(
        shards,
        mesh=mesh,
        in_specs=(
            P("node", "local", None, None, None),
            P("node", "local", None),
            P("node", "local"),
            owned,
            owned,
            owned,
        ),
        out_specs=(owned,) * 4,
        check_vma=False,
    )
```

```python
import functools

import jax
import jax.numpy as jnp
from jax import lax
from jax.experimental import pallas as pl
from jax.experimental.pallas import tpu as pltpu
from jax.sharding import PartitionSpec as P

beta_one = 0.9
beta_two = 0.999
learning_rate = 0.01
correction_one = 1.0 - 0.9**20
correction_two = 1.0 - 0.999**20

LANES = 128
TILE_ROWS = 16
ROUNDER = 1.5 * 2.0**23


def nearest_even(scaled):
    lifted = jnp.floor(scaled + 0.5)
    halfway = lifted - scaled == 0.5
    parity = lifted - 2.0 * jnp.floor(lifted * 0.5)
    return jnp.where(halfway & (parity == 1.0), lifted - 1.0, lifted)


def encode(values, scales, lowest, highest):
    return jnp.clip(nearest_even(values / scales), lowest, highest)


def adam(grad_sum, param, first_moment, second_moment):
    new_first = beta_one * first_moment + (1.0 - beta_one) * grad_sum
    new_second = beta_two * second_moment + (1.0 - beta_two) * grad_sum * grad_sum
    new_param = param - learning_rate * (new_first / correction_one) / (
        jnp.sqrt(new_second / correction_two) + 1e-08
    )
    return new_param, new_first, new_second


def plain_sum(grads, first_scales, second_scales, owned_blocks, block_size):
    locals_count = lax.axis_size("local")
    nodes_count = lax.axis_size("node")
    values = grads.astype(jnp.float32).reshape(locals_count, nodes_count, owned_blocks, block_size)
    scale_one = first_scales.astype(jnp.float32).reshape(locals_count, nodes_count, owned_blocks, 1)
    sent_terms = (encode(values, scale_one, -8.0, 7.0) * scale_one).astype(jnp.bfloat16)
    scale_two = second_scales.astype(jnp.float32).reshape(nodes_count, owned_blocks, 1)
    partial_value = jnp.sum(
        lax.all_to_all(sent_terms, "local", split_axis=0, concat_axis=0, tiled=True).astype(
            jnp.float32
        ),
        axis=0,
    )
    second_terms = (encode(partial_value, scale_two, -127.0, 127.0) * scale_two).astype(
        jnp.bfloat16
    )
    summed = lax.psum_scatter(second_terms, "node", scatter_dimension=0, tiled=True)
    return summed[0].astype(jnp.float32)


def round_to(values, scale, lowest, highest):
    big = scale * ROUNDER
    return jnp.clip((values + big) - big, scale * lowest, scale * highest)


def unfold(flat, first_row, columns, target):
    lane = lax.broadcasted_iota(jnp.int32, (1, LANES), 1)
    width = flat.shape[-1]

    def tile(a):
        held = flat[:, a * LANES : min((a + 1) * LANES, width)].astype(jnp.float32)
        short = LANES - held.shape[-1]
        return jnp.concatenate([held, jnp.zeros((1, short), jnp.float32)], 1) if short else held

    for r in range(TILE_ROWS):
        a, offset = divmod((first_row + r) * columns, LANES)
        row = tile(a)
        if offset:
            row = pltpu.roll(row, LANES - offset, 1)
        if offset + columns > LANES:
            after = pltpu.roll(tile(a + 1), LANES - offset, 1)
            row = jnp.where(lane < LANES - offset, row, after)
        target[r : r + 1, :] = row


def pieces_of(columns):
    fours = columns // 4
    shares = SHARES if fours >= sum(SHARES) else (1,)
    sizes = [fours * share // sum(shares) for share in shares]
    sizes[0] += fours - sum(sizes)
    sizes = [4 * size for size in sizes]
    starts = [sum(sizes[:i]) for i in range(len(sizes))]
    return list(zip(starts, sizes))


SHARES = (11, 10, 8)


def reduce_kernel(
    pieces,
    grads_ref,
    flat_one_ref,
    flat_two_ref,
    out_ref,
    loaded,
    flat_one,
    flat_two,
    scale_one_ref,
    scale_two_ref,
    cross_out,
    cross_in,
    sums,
    joined_in,
    near_in,
    far_in,
    node_out,
    node_in,
    scale_sem,
    load_sem,
    cross_send,
    cross_recv,
    half_send,
    joined_recv,
    near_recv,
    far_send,
    far_recv,
    node_send,
    node_recv,
):
    node = lax.axis_index("node")
    local = lax.axis_index("local")
    z, core = local // 2, local % 2
    half = z // 2
    inner = (z + half) % 2 == 1
    partner = z + 1 - 2 * (z % 2)
    other_inner, other_outer = 2 - half, 3 - 3 * half
    nodes = lax.axis_size("node")
    columns_of = grads_ref.shape[-1] // LANES
    count = len(pieces)

    def at(z_to, core_to, node_to=None):
        return (node if node_to is None else node_to, 2 * z_to + core_to)

    def destination(order):
        return jnp.where(
            order == 0,
            other_outer,
            jnp.where(order == 1, other_inner, jnp.where(order == 2, partner, z)),
        )

    def lanes(p):
        start, size = pieces[p]
        return pl.ds(start * LANES, size * LANES)

    def quarter(p):
        start, size = pieces[p]
        return pl.ds(start // 4 * LANES, size // 4 * LANES)

    barrier = pltpu.get_barrier_semaphore()
    peers = [at(z, 1 - core)]
    peers += [at((z + k) % 4, core) for k in range(1, 4)]
    peers += [(lax.rem(node + k, nodes), local) for k in range(1, 4)]
    for peer in peers:
        pl.semaphore_signal(barrier, inc=1, device_id=peer, device_id_type=pl.DeviceIdType.MESH)

    def load(order, p):
        z_to = destination(order)
        return pltpu.make_async_copy(
            grads_ref.at[pl.ds(2 * z_to, 2), :, lanes(p)],
            loaded.at[order, :, :, lanes(p)],
            load_sem.at[order, p],
        )

    flat_copies = [
        pltpu.make_async_copy(flat_one_ref, flat_one, scale_sem.at[0]),
        pltpu.make_async_copy(flat_two_ref, flat_two, scale_sem.at[1]),
    ]
    flat_copies[0].start()
    for order in range(4):
        for p in range(count):
            load(order, p).start()
    flat_copies[1].start()

    flat_copies[0].wait()
    for chunk in range(scale_one_ref.shape[0]):
        unfold(flat_one, chunk * TILE_ROWS, columns_of, scale_one_ref.at[chunk])

    def cross(order, p):
        return pltpu.make_async_remote_copy(
            src_ref=cross_out.at[order, :, lanes(p)],
            dst_ref=cross_in.at[order, :, lanes(p)],
            send_sem=cross_send.at[order, p],
            recv_sem=cross_recv.at[order, p],
            device_id=at(z, 1 - core),
            device_id_type=pl.DeviceIdType.MESH,
        )

    def to_join(order, p):
        return pltpu.make_async_remote_copy(
            src_ref=sums.at[order, :, lanes(p)],
            dst_ref=joined_in.at[order, :, lanes(p)],
            send_sem=half_send.at[order, p],
            recv_sem=joined_recv.at[order, p],
            device_id=at(partner, core),
            device_id_type=pl.DeviceIdType.MESH,
        )

    def to_near(p):
        return pltpu.make_async_remote_copy(
            src_ref=sums.at[2, :, lanes(p)],
            dst_ref=near_in.at[:, lanes(p)],
            send_sem=half_send.at[2, p],
            recv_sem=near_recv.at[p],
            device_id=at(partner, core),
            device_id_type=pl.DeviceIdType.MESH,
        )

    def to_far(order, p):
        return pltpu.make_async_remote_copy(
            src_ref=sums.at[order, :, lanes(p)],
            dst_ref=far_in.at[:, lanes(p)],
            send_sem=far_send.at[order, p],
            recv_sem=far_recv.at[p],
            device_id=at(destination(order), core),
            device_id_type=pl.DeviceIdType.MESH,
        )

    def to_node(k, p):
        other = lax.rem(node + k, nodes)
        return pltpu.make_async_remote_copy(
            src_ref=node_out.at[other, :, quarter(p)],
            dst_ref=node_in.at[k - 1, :, quarter(p)],
            send_sem=node_send.at[k - 1, p],
            recv_sem=node_recv.at[k - 1, p],
            device_id=(other, local),
            device_id_type=pl.DeviceIdType.MESH,
        )

    def code(order, p, core_to, target):
        chunk = 2 * destination(order) + core_to
        start, size = pieces[p]
        scales = scale_one_ref[chunk]
        for j in range(start, start + size):
            cols = slice(j * LANES, (j + 1) * LANES)
            scale = jnp.broadcast_to(scales[:, j : j + 1], (TILE_ROWS, LANES))
            values = loaded[order, core_to, :, cols].astype(jnp.float32)
            target[order, :, cols] = round_to(values, scale, -8.0, 7.0).astype(jnp.bfloat16)

    def pair_sum(order, p):
        cross(order, p).wait_recv()
        start, size = pieces[p]
        sums[order, :, lanes(p)] = (
            sums[order, :, lanes(p)].astype(jnp.float32)
            + cross_in[order, :, lanes(p)].astype(jnp.float32)
        ).astype(jnp.bfloat16)

        @pl.when(jnp.logical_and(order < 2, jnp.logical_not(inner)))
        def _():
            to_join(order, p).start()

        @pl.when(order == 2)
        def _():
            to_near(p).start()

    def first_phase(order, carry):
        for p in range(count):
            load(order, p).wait()
            code(order, p, 1 - core, cross_out)
            if p == 0:

                @pl.when(order == 0)
                def _():
                    pl.semaphore_wait(barrier, len(peers))

            cross(order, p).start()
            code(order, p, core, sums)

            @pl.when(order > 0)
            def _(p=p):
                pair_sum(order - 1, p)

        return carry

    lax.fori_loop(0, 4, first_phase, 0)
    for p in range(count):
        pair_sum(3, p)

    @pl.when(inner)
    def _():
        for order in range(2):
            for p in range(count):
                to_join(order, p).wait_recv()
                sums[order, :, lanes(p)] = (
                    sums[order, :, lanes(p)].astype(jnp.float32)
                    + joined_in[order, :, lanes(p)].astype(jnp.float32)
                ).astype(jnp.bfloat16)
                to_far(order, p).start()

    flat_copies[1].wait()
    unfold(flat_two, 0, columns_of, scale_two_ref)
    scales_two = scale_two_ref[...]

    def recode(p):
        to_far(0, p).wait_recv()
        to_near(p).wait_recv()
        start, size = pieces[p]
        step = size // 4
        for k in range(step):
            terms = []
            for q in range(4):
                j = start + q * step + k
                cols = slice(j * LANES, (j + 1) * LANES)
                scale = jnp.broadcast_to(scales_two[:, j : j + 1], (TILE_ROWS, LANES))
                total = (
                    sums[3, :, cols].astype(jnp.float32)
                    + near_in[:, cols].astype(jnp.float32)
                    + far_in[:, cols].astype(jnp.float32)
                )
                terms.append(round_to(total, scale, -127.0, 127.0))
            where = slice((start // 4 + k) * LANES, (start // 4 + k + 1) * LANES)
            for n in range(4):
                node_out[n, :, where] = jnp.concatenate(
                    [term[4 * n : 4 * n + 4] for term in terms], axis=0
                ).astype(jnp.bfloat16)
        for k in range(1, 4):
            to_node(k, p).start()

    def collect(p):
        for k in range(1, 4):
            to_node(k, p).wait_recv()
        start, size = pieces[p]
        step = size // 4
        for k in range(step):
            where = slice((start // 4 + k) * LANES, (start // 4 + k + 1) * LANES)
            total = node_out[node, :, where].astype(jnp.float32)
            for i in range(3):
                total = total + node_in[i, :, where].astype(jnp.float32)
            for q in range(4):
                j = start + q * step + k
                out_ref[pl.ds(j, 4, stride=columns_of), :] = total[4 * q : 4 * q + 4]

    for p in range(count):
        recode(p)
        if p > 0:
            collect(p - 1)
    collect(count - 1)

    for p in range(count):
        for order in range(4):
            cross(order, p).wait_send()
        to_near(p).wait_send()
        for k in range(1, 4):
            to_node(k, p).wait_send()

    @pl.when(inner)
    def _():
        for p in range(count):
            for order in range(2):
                to_far(order, p).wait_send()

    @pl.when(jnp.logical_not(inner))
    def _():
        for p in range(count):
            for order in range(2):
                to_join(order, p).wait_send()


def line_sum(grads, first_scales, second_scales, owned_blocks, block_size):
    locals_count = lax.axis_size("local")
    depth = grads.shape[-1]
    pieces = pieces_of(depth // block_size)
    count = len(pieces)
    rows = TILE_ROWS
    scratch = [
        pltpu.VMEM((4, 2, rows, depth), jnp.bfloat16),
        pltpu.VMEM((1, first_scales.shape[-1]), jnp.bfloat16),
        pltpu.VMEM((1, second_scales.shape[-1]), jnp.bfloat16),
        pltpu.VMEM((locals_count, rows, LANES), jnp.float32),
        pltpu.VMEM((rows, LANES), jnp.float32),
        pltpu.VMEM((4, rows, depth), jnp.bfloat16),
        pltpu.VMEM((4, rows, depth), jnp.bfloat16),
        pltpu.VMEM((4, rows, depth), jnp.bfloat16),
        pltpu.VMEM((2, rows, depth), jnp.bfloat16),
        pltpu.VMEM((rows, depth), jnp.bfloat16),
        pltpu.VMEM((rows, depth), jnp.bfloat16),
        pltpu.VMEM((4, rows, depth // 4), jnp.bfloat16),
        pltpu.VMEM((3, rows, depth // 4), jnp.bfloat16),
    ]
    sems = [(2,)] + [(4, count)] * 3
    sems += [(3, count), (2, count), (count,), (2, count), (count,), (3, count), (3, count)]
    return pl.pallas_call(
        functools.partial(reduce_kernel, pieces),
        out_shape=jax.ShapeDtypeStruct((owned_blocks, block_size), jnp.float32),
        in_specs=[
            pl.BlockSpec(memory_space=pl.ANY),
            pl.BlockSpec(memory_space=pl.ANY),
            pl.BlockSpec(memory_space=pl.ANY),
        ],
        out_specs=pl.BlockSpec(memory_space=pltpu.VMEM),
        scratch_shapes=scratch + [pltpu.SemaphoreType.DMA(shape) for shape in sems],
        compiler_params=pltpu.CompilerParams(
            collective_id=0, has_side_effects=True, vmem_limit_bytes=61 * 2**20
        ),
    )(
        grads.reshape(locals_count, rows, depth),
        first_scales.reshape(1, -1),
        second_scales,
    )


def adam_kernel(reduced, param, first, second, grad_sum, new_param, new_first, new_second):
    total = reduced[...]
    grad_sum[...] = total
    new_param[...], new_first[...], new_second[...] = adam(
        total, param[...], first[...], second[...]
    )


def finish(reduced, param, first_moment, second_moment):
    shape = reduced.shape
    steps = 2 if shape[0] % 16 == 0 else 1
    block = pl.BlockSpec((shape[0] // steps, shape[1]), lambda i: (i, 0))
    return pl.pallas_call(
        adam_kernel,
        out_shape=[jax.ShapeDtypeStruct(shape, jnp.float32)] * 4,
        grid=(steps,),
        in_specs=[block] * 4,
        out_specs=[block] * 4,
        cost_estimate=pl.CostEstimate(
            flops=16 * reduced.size, bytes_accessed=32 * reduced.size, transcendentals=reduced.size
        ),
    )(reduced, param.reshape(shape), first_moment.reshape(shape), second_moment.reshape(shape))


def shards(grads, first_scales, second_scales, param, first_moment, second_moment):
    owned_blocks, block_size = param.shape[2:]
    nodes_count, locals_count = lax.axis_size("node"), lax.axis_size("local")
    depth = grads.shape[-1]
    columns = depth // block_size
    fits = (
        nodes_count == 4
        and locals_count == 8
        and block_size == LANES
        and depth % block_size == 0
        and columns % 4 == 0
        and owned_blocks == 4 * columns
        and grads.shape[-2] % TILE_ROWS == 0
    )
    if fits:
        reduced = line_sum(grads, first_scales, second_scales, owned_blocks, block_size)
        outputs = finish(reduced, param, first_moment, second_moment)
        return tuple(output.reshape(param.shape) for output in outputs)
    grad_sum = plain_sum(grads, first_scales, second_scales, owned_blocks, block_size)
    grad_sum = grad_sum.reshape(param.shape)
    return (grad_sum, *adam(grad_sum, param, first_moment, second_moment))


def solution(mesh):
    owned = P("local", "node", None, None)
    return jax.shard_map(
        shards,
        mesh=mesh,
        in_specs=(
            P("node", "local", None, None, None),
            P("node", "local", None),
            P("node", "local"),
            owned,
            owned,
            owned,
        ),
        out_specs=(owned,) * 4,
        check_vma=False,
    )
```

```python
import functools

import jax
import jax.numpy as jnp
from jax import lax
from jax.experimental import pallas as pl
from jax.experimental.pallas import tpu as pltpu
from jax.sharding import PartitionSpec as P

beta_one = 0.9
beta_two = 0.999
learning_rate = 0.01
correction_one = 1.0 - 0.9**20
correction_two = 1.0 - 0.999**20

LANES = 128
TILE_ROWS = 16
ROUNDER = 1.5 * 2.0**23


def nearest_even(scaled):
    lifted = jnp.floor(scaled + 0.5)
    halfway = lifted - scaled == 0.5
    parity = lifted - 2.0 * jnp.floor(lifted * 0.5)
    return jnp.where(halfway & (parity == 1.0), lifted - 1.0, lifted)


def encode(values, scales, lowest, highest):
    return jnp.clip(nearest_even(values / scales), lowest, highest)


def adam(grad_sum, param, first_moment, second_moment):
    new_first = beta_one * first_moment + (1.0 - beta_one) * grad_sum
    new_second = beta_two * second_moment + (1.0 - beta_two) * grad_sum * grad_sum
    new_param = param - learning_rate * (new_first / correction_one) / (
        jnp.sqrt(new_second / correction_two) + 1e-08
    )
    return new_param, new_first, new_second


def plain_sum(grads, first_scales, second_scales, owned_blocks, block_size):
    locals_count = lax.axis_size("local")
    nodes_count = lax.axis_size("node")
    values = grads.astype(jnp.float32).reshape(locals_count, nodes_count, owned_blocks, block_size)
    scale_one = first_scales.astype(jnp.float32).reshape(locals_count, nodes_count, owned_blocks, 1)
    sent_terms = (encode(values, scale_one, -8.0, 7.0) * scale_one).astype(jnp.bfloat16)
    scale_two = second_scales.astype(jnp.float32).reshape(nodes_count, owned_blocks, 1)
    partial_value = jnp.sum(
        lax.all_to_all(sent_terms, "local", split_axis=0, concat_axis=0, tiled=True).astype(
            jnp.float32
        ),
        axis=0,
    )
    second_terms = (encode(partial_value, scale_two, -127.0, 127.0) * scale_two).astype(
        jnp.bfloat16
    )
    summed = lax.psum_scatter(second_terms, "node", scatter_dimension=0, tiled=True)
    return summed[0].astype(jnp.float32)


def round_to(values, scale, lowest, highest):
    big = scale * ROUNDER
    return jnp.clip((values + big) - big, scale * lowest, scale * highest)


def unfold(flat, first_row, columns, target):
    lane = lax.broadcasted_iota(jnp.int32, (1, LANES), 1)
    width = flat.shape[-1]

    def tile(a):
        held = flat[:, a * LANES : min((a + 1) * LANES, width)].astype(jnp.float32)
        short = LANES - held.shape[-1]
        return jnp.concatenate([held, jnp.zeros((1, short), jnp.float32)], 1) if short else held

    for r in range(TILE_ROWS):
        a, offset = divmod((first_row + r) * columns, LANES)
        row = tile(a)
        if offset:
            row = pltpu.roll(row, LANES - offset, 1)
        if offset + columns > LANES:
            after = pltpu.roll(tile(a + 1), LANES - offset, 1)
            row = jnp.where(lane < LANES - offset, row, after)
        target[r : r + 1, :] = row


def pieces_of(columns):
    fours = columns // 4
    shares = SHARES if fours >= sum(SHARES) else (1,)
    sizes = [fours * share // sum(shares) for share in shares]
    sizes[0] += fours - sum(sizes)
    sizes = [4 * size for size in sizes]
    starts = [sum(sizes[:i]) for i in range(len(sizes))]
    return list(zip(starts, sizes))


SHARES = (11, 10, 8)


def reduce_kernel(
    pieces,
    grads_ref,
    flat_one_ref,
    flat_two_ref,
    out_ref,
    loaded,
    flat_one,
    flat_two,
    scale_one_ref,
    scale_two_ref,
    cross_out,
    cross_in,
    sums,
    joined_in,
    near_in,
    far_in,
    node_out,
    node_in,
    scale_sem,
    load_sem,
    cross_send,
    cross_recv,
    half_send,
    joined_recv,
    near_recv,
    far_send,
    far_recv,
    node_send,
    node_recv,
):
    node = lax.axis_index("node")
    local = lax.axis_index("local")
    z, core = local // 2, local % 2
    half = z // 2
    inner = (z + half) % 2 == 1
    partner = z + 1 - 2 * (z % 2)
    other_inner, other_outer = 2 - half, 3 - 3 * half
    nodes = lax.axis_size("node")
    columns_of = grads_ref.shape[-1] // LANES
    count = len(pieces)

    def at(z_to, core_to, node_to=None):
        return (node if node_to is None else node_to, 2 * z_to + core_to)

    def destination(order):
        return jnp.where(
            order == 0,
            other_outer,
            jnp.where(order == 1, other_inner, jnp.where(order == 2, partner, z)),
        )

    def lanes(p):
        start, size = pieces[p]
        return pl.ds(start * LANES, size * LANES)

    def quarter(p):
        start, size = pieces[p]
        return pl.ds(start // 4 * LANES, size // 4 * LANES)

    barrier = pltpu.get_barrier_semaphore()
    peers = [at(z, 1 - core)]
    peers += [at((z + k) % 4, core) for k in range(1, 4)]
    peers += [(lax.rem(node + k, nodes), local) for k in range(1, 4)]
    for peer in peers:
        pl.semaphore_signal(barrier, inc=1, device_id=peer, device_id_type=pl.DeviceIdType.MESH)

    def load(order, p):
        z_to = destination(order)
        return pltpu.make_async_copy(
            grads_ref.at[pl.ds(2 * z_to, 2), :, lanes(p)],
            loaded.at[order, :, :, lanes(p)],
            load_sem.at[order, p],
        )

    flat_copies = [
        pltpu.make_async_copy(flat_one_ref, flat_one, scale_sem.at[0]),
        pltpu.make_async_copy(flat_two_ref, flat_two, scale_sem.at[1]),
    ]
    flat_copies[0].start()
    for order in range(4):
        for p in range(count):
            load(order, p).start()
    flat_copies[1].start()

    flat_copies[0].wait()

    def cross(order, p):
        return pltpu.make_async_remote_copy(
            src_ref=cross_out.at[order, :, lanes(p)],
            dst_ref=cross_in.at[order, :, lanes(p)],
            send_sem=cross_send.at[order, p],
            recv_sem=cross_recv.at[order, p],
            device_id=at(z, 1 - core),
            device_id_type=pl.DeviceIdType.MESH,
        )

    def to_join(order, p):
        return pltpu.make_async_remote_copy(
            src_ref=sums.at[order, :, lanes(p)],
            dst_ref=joined_in.at[order, :, lanes(p)],
            send_sem=half_send.at[order, p],
            recv_sem=joined_recv.at[order, p],
            device_id=at(partner, core),
            device_id_type=pl.DeviceIdType.MESH,
        )

    def to_near(p):
        return pltpu.make_async_remote_copy(
            src_ref=sums.at[2, :, lanes(p)],
            dst_ref=near_in.at[:, lanes(p)],
            send_sem=half_send.at[2, p],
            recv_sem=near_recv.at[p],
            device_id=at(partner, core),
            device_id_type=pl.DeviceIdType.MESH,
        )

    def to_far(order, p):
        return pltpu.make_async_remote_copy(
            src_ref=sums.at[order, :, lanes(p)],
            dst_ref=far_in.at[:, lanes(p)],
            send_sem=far_send.at[order, p],
            recv_sem=far_recv.at[p],
            device_id=at(destination(order), core),
            device_id_type=pl.DeviceIdType.MESH,
        )

    def to_node(k, p):
        other = lax.rem(node + k, nodes)
        return pltpu.make_async_remote_copy(
            src_ref=node_out.at[other, :, quarter(p)],
            dst_ref=node_in.at[k - 1, :, quarter(p)],
            send_sem=node_send.at[k - 1, p],
            recv_sem=node_recv.at[k - 1, p],
            device_id=(other, local),
            device_id_type=pl.DeviceIdType.MESH,
        )

    def code(order, p, core_to, target):
        chunk = 2 * destination(order) + core_to
        start, size = pieces[p]
        scales = scale_one_ref[chunk]
        for j in range(start, start + size):
            cols = slice(j * LANES, (j + 1) * LANES)
            scale = jnp.broadcast_to(scales[:, j : j + 1], (TILE_ROWS, LANES))
            values = loaded[order, core_to, :, cols].astype(jnp.float32)
            target[order, :, cols] = round_to(values, scale, -8.0, 7.0).astype(jnp.bfloat16)

    def pair_sum(order, p):
        cross(order, p).wait_recv()
        start, size = pieces[p]
        sums[order, :, lanes(p)] = (
            sums[order, :, lanes(p)].astype(jnp.float32)
            + cross_in[order, :, lanes(p)].astype(jnp.float32)
        ).astype(jnp.bfloat16)

        @pl.when(jnp.logical_and(order < 2, jnp.logical_not(inner)))
        def _():
            to_join(order, p).start()

        @pl.when(order == 2)
        def _():
            to_near(p).start()

    def first_phase(order, carry):
        for z_to in range(scale_one_ref.shape[0] // 2):

            @pl.when(destination(order) == z_to)
            def _(z_to=z_to):
                for chunk in (2 * z_to, 2 * z_to + 1):
                    unfold(flat_one, chunk * TILE_ROWS, columns_of, scale_one_ref.at[chunk])

        for p in range(count):
            load(order, p).wait()
            code(order, p, 1 - core, cross_out)
            if p == 0:

                @pl.when(order == 0)
                def _():
                    pl.semaphore_wait(barrier, len(peers))

            cross(order, p).start()
            code(order, p, core, sums)

            @pl.when(order > 0)
            def _(p=p):
                pair_sum(order - 1, p)

        return carry

    lax.fori_loop(0, 4, first_phase, 0)
    for p in range(count):
        pair_sum(3, p)

    @pl.when(inner)
    def _():
        for order in range(2):
            for p in range(count):
                to_join(order, p).wait_recv()
                sums[order, :, lanes(p)] = (
                    sums[order, :, lanes(p)].astype(jnp.float32)
                    + joined_in[order, :, lanes(p)].astype(jnp.float32)
                ).astype(jnp.bfloat16)
                to_far(order, p).start()

    flat_copies[1].wait()
    unfold(flat_two, 0, columns_of, scale_two_ref)
    scales_two = scale_two_ref[...]

    def recode(p):
        to_far(0, p).wait_recv()
        to_near(p).wait_recv()
        start, size = pieces[p]
        step = size // 4
        for k in range(step):
            terms = []
            for q in range(4):
                j = start + q * step + k
                cols = slice(j * LANES, (j + 1) * LANES)
                scale = jnp.broadcast_to(scales_two[:, j : j + 1], (TILE_ROWS, LANES))
                total = (
                    sums[3, :, cols].astype(jnp.float32)
                    + near_in[:, cols].astype(jnp.float32)
                    + far_in[:, cols].astype(jnp.float32)
                )
                terms.append(round_to(total, scale, -127.0, 127.0))
            where = slice((start // 4 + k) * LANES, (start // 4 + k + 1) * LANES)
            for n in range(4):
                node_out[n, :, where] = jnp.concatenate(
                    [term[4 * n : 4 * n + 4] for term in terms], axis=0
                ).astype(jnp.bfloat16)
        for k in range(1, 4):
            to_node(k, p).start()

    def collect(p):
        for k in range(1, 4):
            to_node(k, p).wait_recv()
        start, size = pieces[p]
        step = size // 4
        for k in range(step):
            where = slice((start // 4 + k) * LANES, (start // 4 + k + 1) * LANES)
            total = node_out[node, :, where].astype(jnp.float32)
            for i in range(3):
                total = total + node_in[i, :, where].astype(jnp.float32)
            for q in range(4):
                j = start + q * step + k
                out_ref[pl.ds(j, 4, stride=columns_of), :] = total[4 * q : 4 * q + 4]

    for p in range(count):
        recode(p)
        if p > 0:
            collect(p - 1)
    collect(count - 1)

    for p in range(count):
        for order in range(4):
            cross(order, p).wait_send()
        to_near(p).wait_send()
        for k in range(1, 4):
            to_node(k, p).wait_send()

    @pl.when(inner)
    def _():
        for p in range(count):
            for order in range(2):
                to_far(order, p).wait_send()

    @pl.when(jnp.logical_not(inner))
    def _():
        for p in range(count):
            for order in range(2):
                to_join(order, p).wait_send()


def line_sum(grads, first_scales, second_scales, owned_blocks, block_size):
    locals_count = lax.axis_size("local")
    depth = grads.shape[-1]
    pieces = pieces_of(depth // block_size)
    count = len(pieces)
    rows = TILE_ROWS
    scratch = [
        pltpu.VMEM((4, 2, rows, depth), jnp.bfloat16),
        pltpu.VMEM((1, first_scales.shape[-1]), jnp.bfloat16),
        pltpu.VMEM((1, second_scales.shape[-1]), jnp.bfloat16),
        pltpu.VMEM((locals_count, rows, LANES), jnp.float32),
        pltpu.VMEM((rows, LANES), jnp.float32),
        pltpu.VMEM((4, rows, depth), jnp.bfloat16),
        pltpu.VMEM((4, rows, depth), jnp.bfloat16),
        pltpu.VMEM((4, rows, depth), jnp.bfloat16),
        pltpu.VMEM((2, rows, depth), jnp.bfloat16),
        pltpu.VMEM((rows, depth), jnp.bfloat16),
        pltpu.VMEM((rows, depth), jnp.bfloat16),
        pltpu.VMEM((4, rows, depth // 4), jnp.bfloat16),
        pltpu.VMEM((3, rows, depth // 4), jnp.bfloat16),
    ]
    sems = [(2,)] + [(4, count)] * 3
    sems += [(3, count), (2, count), (count,), (2, count), (count,), (3, count), (3, count)]
    return pl.pallas_call(
        functools.partial(reduce_kernel, pieces),
        out_shape=jax.ShapeDtypeStruct((owned_blocks, block_size), jnp.float32),
        in_specs=[
            pl.BlockSpec(memory_space=pl.ANY),
            pl.BlockSpec(memory_space=pl.ANY),
            pl.BlockSpec(memory_space=pl.ANY),
        ],
        out_specs=pl.BlockSpec(memory_space=pltpu.VMEM),
        scratch_shapes=scratch + [pltpu.SemaphoreType.DMA(shape) for shape in sems],
        compiler_params=pltpu.CompilerParams(
            collective_id=0, has_side_effects=True, vmem_limit_bytes=61 * 2**20
        ),
    )(
        grads.reshape(locals_count, rows, depth),
        first_scales.reshape(1, -1),
        second_scales,
    )


def adam_kernel(reduced, param, first, second, grad_sum, new_param, new_first, new_second):
    total = reduced[...]
    grad_sum[...] = total
    new_param[...], new_first[...], new_second[...] = adam(
        total, param[...], first[...], second[...]
    )


def finish(reduced, param, first_moment, second_moment):
    shape = reduced.shape
    steps = 2 if shape[0] % 16 == 0 else 1
    block = pl.BlockSpec((shape[0] // steps, shape[1]), lambda i: (i, 0))
    return pl.pallas_call(
        adam_kernel,
        out_shape=[jax.ShapeDtypeStruct(shape, jnp.float32)] * 4,
        grid=(steps,),
        in_specs=[block] * 4,
        out_specs=[block] * 4,
        cost_estimate=pl.CostEstimate(
            flops=16 * reduced.size, bytes_accessed=32 * reduced.size, transcendentals=reduced.size
        ),
    )(reduced, param.reshape(shape), first_moment.reshape(shape), second_moment.reshape(shape))


def shards(grads, first_scales, second_scales, param, first_moment, second_moment):
    owned_blocks, block_size = param.shape[2:]
    nodes_count, locals_count = lax.axis_size("node"), lax.axis_size("local")
    depth = grads.shape[-1]
    columns = depth // block_size
    fits = (
        nodes_count == 4
        and locals_count == 8
        and block_size == LANES
        and depth % block_size == 0
        and columns % 4 == 0
        and owned_blocks == 4 * columns
        and grads.shape[-2] % TILE_ROWS == 0
    )
    if fits:
        reduced = line_sum(grads, first_scales, second_scales, owned_blocks, block_size)
        outputs = finish(reduced, param, first_moment, second_moment)
        return tuple(output.reshape(param.shape) for output in outputs)
    grad_sum = plain_sum(grads, first_scales, second_scales, owned_blocks, block_size)
    grad_sum = grad_sum.reshape(param.shape)
    return (grad_sum, *adam(grad_sum, param, first_moment, second_moment))


def solution(mesh):
    owned = P("local", "node", None, None)
    return jax.shard_map(
        shards,
        mesh=mesh,
        in_specs=(
            P("node", "local", None, None, None),
            P("node", "local", None),
            P("node", "local"),
            owned,
            owned,
            owned,
        ),
        out_specs=(owned,) * 4,
        check_vma=False,
    )
```
